32 devices in a mesh: tm: 16 (over z, x, core), space: 2 (over y).
Axes of the slice: x: 2, y: 2, z: 4, core: 2. Of those that a mesh axis runs over, the one named last changes fastest.
Arguments:
- primal: float32 [128, 5, 16, 16, 128], P('tm', None, 'space'), may hold values from -2 to 2
- source: float32 [128, 5, 16, 16, 128], P('tm', None, 'space'), may hold values from -4 to 4
- guess: float32 [16, 5, 16, 16, 128], P('tm', None, 'space'), may hold values from -6 to 6
- mixing: float32 [5, 5], replicated, may hold values from -1 to 1.2
Outputs:
- fine_states: float32 [128, 5, 16, 16, 128], P('tm', None, 'space')
- coarse_residual: float32 [16, 5, 16, 16, 128], P('tm', None, 'space')
The draws below stay inside these ranges and needn't reach their ends.
All inputs are finite; a program needn't handle non-finite values.
Results may differ from the reference program's by a relative error of at most 0.00026.
Values sent between devices are 32-bit elements; how exact they have to be, the bound alone decides.
A program may use at most 64 MiB of HBM per device.

```python
import jax
import jax.numpy as jnp
from jax import lax

FIELDS = 5
STEPS = 8
NY = 16
NZ = 128
NX = 16
BLOCKS = 16
NT = 128
N_TM = 16


def draw_mixing(key, part):
    keys = jax.random.split(jax.random.fold_in(key, 7), 4)
    order = jax.random.permutation(keys[0], FIELDS)
    slow_count = (FIELDS + 1) // 2
    slow_mask = (order < slow_count).astype(jnp.float32)
    slow_diag = jax.random.uniform(keys[1], (FIELDS,), jnp.float32, 1.02, 1.12)
    fast_diag = jax.random.uniform(keys[2], (FIELDS,), jnp.float32, 0.1, 0.35)
    diagonal = slow_mask * slow_diag + (1.0 - slow_mask) * fast_diag
    raw = 0.1 * jax.random.truncated_normal(keys[3], -3.0, 3.0, (FIELDS, FIELDS), jnp.float32)
    turning = raw - raw.T
    return jnp.diag(diagonal) + turning


def shard_levels(stream_key, dims, cuts, smallest, high):
    loudness, own = 1.0, jax.random.fold_in(stream_key, 6)
    for dim, shards_of in cuts:
        heights = jnp.exp(jax.random.uniform(jax.random.fold_in(own, dim), (shards_of,), jnp.float32, smallest / len(cuts), high / len(cuts)))
        loudness = loudness * jnp.repeat(heights, dims[dim] // shards_of).reshape([-1 if axis == dim else 1 for axis in range(len(dims))])
    return loudness


def normal_values(own_key, extent, scale, bound, pieces=(), kind=jnp.bfloat16):
    values = jax.random.normal(own_key, extent, jnp.float32) * scale
    if len(pieces) > 0:
        values = shard_levels(own_key, extent, pieces, -0.22, 0.18) * values
    return jnp.clip(values, min=-bound, max=bound).astype(kind)


def setup_inputs(seed: int = 0) -> dict:
    splits = jax.random.split(jax.random.key(seed), 5)
    primal = normal_values(splits[0], (NT, FIELDS, NX, NY, NZ), 0.35, 2.0, ((0, 16), (2, 2)), jnp.float32)
    source = normal_values(splits[1], (NT, FIELDS, NX, NY, NZ), 0.5, 4.0, ((0, 16), (2, 2)), jnp.float32)
    guess = normal_values(splits[2], (BLOCKS, FIELDS, NX, NY, NZ), 1.0, 6.0, ((0, 16), (2, 2)), jnp.float32)
    mixing = draw_mixing(jax.random.fold_in(splits[4], 71), 0)
    return dict(primal=primal, source=source, guess=guess, mixing=mixing)


DIFFUSION = 0.1
RATE = 0.25
COARSE_STEP = 0.75


def apply_mix(mixing, field):
    return jnp.einsum("ij,...jxyz->...ixyz", mixing, field, precision=lax.Precision.HIGHEST)


def slopes(mixing, state):
    tilted = jnp.tanh(apply_mix(mixing, state))
    return 1.0 - tilted * tilted


def laplace(field, across):
    widths = [(0, 0)] * (field.ndim - 2) + [(1, 1), (0, 0)]
    padded = jnp.pad(field, widths)
    total = across + padded[..., 2:, :] + padded[..., :-2, :]
    total = total + jnp.roll(field, 1, -1) + jnp.roll(field, -1, -1)
    return total - 6.0 * field


def advance(mixing, state, field, across):
    return field + DIFFUSION * laplace(field, across) + RATE * (slopes(mixing, state) * apply_mix(mixing, field) - field)


def march(mixing, states, sources, start, count):
    field = start
    marched = []
    for column in range(count):
        across = jnp.roll(field, 1, -3) + jnp.roll(field, -1, -3)
        field = advance(mixing, states[:, column], field, across)
        if column + 1 < STEPS:
            field = field + sources[:, column + 1]
        marched.append(field)
    return marched


def reference(primal, source, guess, mixing):
    shape = (N_TM, STEPS) + primal.shape[1:]
    states = primal.reshape(shape)
    sources = source.reshape(shape)
    ended = march(mixing, states, sources, guess, STEPS)[-1]
    relaxed = jnp.concatenate([guess[:1], ended[:-1] + sources[1:, 0]], axis=0)
    ended_again = march(mixing, states, sources, relaxed, STEPS)[-1]
    residual = jnp.concatenate([sources[:1, 0], ended_again[:-1] + sources[1:, 0] - relaxed[1:]], axis=0)
    coarse_slope = slopes(mixing, states[:, 0])

    def coarse_turn(error, inputs):
        slope_here, resid_next = inputs
        moved = error + COARSE_STEP * (slope_here * apply_mix(mixing, error) - error)
        following = moved + resid_next
        return following, following

    start_error = residual[0]
    last_error, errors = lax.scan(coarse_turn, start_error, (coarse_slope[:-1], residual[1:]))
    errors = jnp.concatenate([start_error[None], errors], axis=0)
    corrected = relaxed + errors
    finals = march(mixing, states, sources, corrected, STEPS - 1)
    fine_states = jnp.stack([corrected] + finals, axis=1).reshape(primal.shape)
    return fine_states, residual
```

```python
import functools

import jax
import jax.numpy as jnp
from jax import lax
from jax.experimental import pallas as pl
from jax.experimental.pallas import tpu as pltpu
from jax.sharding import PartitionSpec as P

DIFFUSION = 0.1
RATE = 0.25
COARSE_STEP = 0.75
KEEP = 1.0 - 6.0 * DIFFUSION - RATE
MESH = pl.DeviceIdType.MESH
LEFT, RIGHT = 0, 1


def kernel(blocks, slabs, primal_hbm, source_hbm, guess, mixing, fine, residual_out,
           primal, source, scaled, state, halo, ends, end_in, relaxed, moved, moved_in,
           load_p, load_s, halo_send, halo_recv, end_send, end_recv, err_send, err_recv):
    steps, fields, nx, ny, nz = primal.shape
    last = nx - 1
    position = lax.axis_index("tm")
    slab = lax.axis_index("space")
    side = {LEFT: lax.rem(slab + slabs - 1, slabs), RIGHT: lax.rem(slab + 1, slabs)}
    edge = {LEFT: 0, RIGHT: last}
    first_block = position == 0
    has_next = position < blocks - 1
    groups = halo_send.shape[-1]
    cuts = [(g * fields) // groups for g in range(groups + 1)]

    def load_primal(t):
        return pltpu.make_async_copy(primal_hbm.at[t], primal.at[t], load_p.at[t])

    def load_source(t):
        return pltpu.make_async_copy(source_hbm.at[t], source.at[t], load_s.at[t])

    load_primal(0).start()
    load_source(0).start()
    for t in range(1, steps):
        load_source(t).start()
        load_primal(t).start()

    barrier = pltpu.get_barrier_semaphore()
    for way in (LEFT, RIGHT):
        pl.semaphore_signal(barrier, inc=1, device_id={"space": side[way]}, device_id_type=MESH)

    @pl.when(has_next)
    def _():
        pl.semaphore_signal(barrier, inc=1, device_id={"tm": position + 1}, device_id_type=MESH)

    @pl.when(jnp.logical_not(first_block))
    def _():
        pl.semaphore_signal(barrier, inc=1, device_id={"tm": position - 1}, device_id_type=MESH)

    pl.semaphore_wait(barrier, 2 + jnp.where(first_block, 0, 1) + jnp.where(has_next, 1, 0))

    weights = [[mixing[i, j] for j in range(fields)] for i in range(fields)]

    def mix(values, i):
        total = weights[i][0] * values[0]
        for j in range(1, fields):
            total = total + weights[i][j] * values[j]
        return total

    rows = lax.broadcasted_iota(jnp.int32, (ny, nz), 0)
    top, bottom = rows == 0, rows == ny - 1

    def halo_copy(way, slot, g):
        part = pl.ds(cuts[g], cuts[g + 1] - cuts[g])
        return pltpu.make_async_remote_copy(
            src_ref=state.at[slot, edge[way], part],
            dst_ref=halo.at[way, slot, part],
            send_sem=halo_send.at[way, slot, g],
            recv_sem=halo_recv.at[way, slot, g],
            device_id={"space": side[way]},
            device_id_type=MESH,
        )

    def end_copy(m, x):
        return pltpu.make_async_remote_copy(
            src_ref=ends.at[m, x], dst_ref=end_in.at[m, x],
            send_sem=end_send.at[m, x], recv_sem=end_recv.at[m, x],
            device_id={"tm": position + 1}, device_id_type=MESH,
        )

    def err_copy(x):
        return pltpu.make_async_remote_copy(
            src_ref=moved.at[x], dst_ref=moved_in.at[x],
            send_sem=err_send.at[x], recv_sem=err_recv.at[x],
            device_id={"tm": position + 1}, device_id_type=MESH,
        )

    def stepped(slot, t, x, near):
        values = [state[slot, x, f] for f in range(fields)]
        results = []
        for f in range(fields):
            v = values[f]
            around = jnp.where(top, 0.0, pltpu.roll(v, 1, 0))
            around = around + jnp.where(bottom, 0.0, pltpu.roll(v, ny - 1, 0))
            around = around + pltpu.roll(v, 1, 1) + pltpu.roll(v, nz - 1, 1)
            for other in near:
                around = around + state[slot, other, f]
            results.append(KEEP * v + DIFFUSION * around + scaled[t, f, x] * mix(values, f))
        return results

    def step(m, slot, t, ways, closing):
        final = m == 2

        def put(x, f, value):
            if closing and not final:
                ends[m, x, f] = value
                return
            value = value + source[t + 1, f, x]
            if final:
                fine[t + 1, f, x] = value
            if not closing:
                state[1 - slot, x, f] = value

        if m == 0:
            load_primal(t).wait()
            if not closing:
                load_source(t + 1).wait()

            def slope(x, carry):
                values = [primal[t, f, x] for f in range(fields)]
                for f in range(fields):
                    bent = jnp.tanh(mix(values, f))
                    scaled[t, f, x] = RATE - RATE * (bent * bent)
                return carry

            lax.fori_loop(0, nx, slope, 0)

        def inner(x, carry):
            results = stepped(slot, t, x, (x - 1, x + 1))
            for f in range(fields):
                put(x, f, results[f])
            if closing and not final:
                @pl.when(has_next)
                def _():
                    end_copy(m, x).start()
            return carry

        lax.fori_loop(1, last, inner, 0)
        for way in ways:
            target = RIGHT if way == LEFT else LEFT
            x = edge[target]
            results = stepped(slot, t, x, (x + 1 if target == LEFT else x - 1,))
            for g in range(groups):
                halo_copy(way, slot, g).wait_recv()
                for f in range(cuts[g], cuts[g + 1]):
                    put(x, f, results[f] + DIFFUSION * halo[way, slot, f])
                if not closing:
                    halo_copy(target, 1 - slot, g).start()
            if closing and not final:
                @pl.when(has_next)
                def _():
                    end_copy(m, x).start()
        for way in ways:
            for g in range(groups):
                halo_copy(way, slot, g).wait_send()

    forward, backward = (LEFT, RIGHT), (RIGHT, LEFT)

    def march(m, count):
        pairs = (count - 1) // 2

        def pair(i, carry):
            step(m, 0, 2 * i, forward, False)
            step(m, 1, 2 * i + 1, backward, False)
            return carry

        lax.fori_loop(0, pairs, pair, 0)
        for t in range(2 * pairs, count):
            step(m, t % 2, t, (forward, backward)[t % 2], t == count - 1)

    def send_edge(way):
        for g in range(groups):
            halo_copy(way, 0, g).start()

    def begin(place):
        place(edge[LEFT])
        send_edge(LEFT)
        place(edge[RIGHT])
        send_edge(RIGHT)

        def rest(x, carry):
            place(x)
            return carry

        lax.fori_loop(1, last, rest, 0)

    def from_guess(x):
        for f in range(fields):
            state[0, x, f] = guess[0, f, x]

    begin(from_guess)
    load_source(0).wait()
    march(0, steps)

    def from_end(x):
        @pl.when(first_block)
        def _():
            for f in range(fields):
                value = guess[0, f, x]
                state[0, x, f] = value
                relaxed[x, f] = value

        @pl.when(jnp.logical_not(first_block))
        def _():
            end_copy(0, x).wait_recv()
            for f in range(fields):
                value = end_in[0, x, f] + source[0, f, x]
                state[0, x, f] = value
                relaxed[x, f] = value

    begin(from_end)
    march(1, steps)

    def from_error(x):
        @pl.when(first_block)
        def _():
            for f in range(fields):
                value = source[0, f, x]
                residual_out[0, f, x] = value
                moved_in[x, f] = value

        @pl.when(jnp.logical_not(first_block))
        def _():
            end_copy(1, x).wait_recv()
            rest = []
            for f in range(fields):
                value = end_in[1, x, f] + source[0, f, x] - relaxed[x, f]
                residual_out[0, f, x] = value
                rest.append(value)
            err_copy(x).wait_recv()
            for f in range(fields):
                moved_in[x, f] = moved_in[x, f] + rest[f]

        error = [moved_in[x, f] for f in range(fields)]

        @pl.when(has_next)
        def _():
            for f in range(fields):
                moved[x, f] = (1.0 - COARSE_STEP) * error[f] + (COARSE_STEP / RATE) * (
                    scaled[0, f, x] * mix(error, f))
            err_copy(x).start()

        for f in range(fields):
            value = relaxed[x, f] + error[f]
            state[0, x, f] = value
            fine[0, f, x] = value

    begin(from_error)
    march(2, steps - 1)

    @pl.when(has_next)
    def _():
        def drain(x, carry):
            end_copy(0, x).wait_send()
            end_copy(1, x).wait_send()
            err_copy(x).wait_send()
            return carry

        lax.fori_loop(0, nx, drain, 0)


def per_device(blocks, slabs, primal, source, guess, mixing):
    steps, fields, nx, ny, nz = primal.shape
    groups = 2
    plane = (nx, fields, ny, nz)
    vmem = pl.BlockSpec(memory_space=pltpu.VMEM)
    dma = pltpu.SemaphoreType.DMA
    f32 = jnp.float32
    return pl.pallas_call(
        functools.partial(kernel, blocks, slabs),
        out_shape=(jax.ShapeDtypeStruct(primal.shape, f32), jax.ShapeDtypeStruct(guess.shape, f32)),
        in_specs=[pl.BlockSpec(memory_space=pl.ANY)] * 2
        + [vmem, pl.BlockSpec(memory_space=pltpu.SMEM)],
        out_specs=(vmem, vmem),
        scratch_shapes=[
            pltpu.VMEM(primal.shape, f32),
            pltpu.VMEM(primal.shape, f32),
            pltpu.VMEM(primal.shape, f32),
            pltpu.VMEM((2,) + plane, f32),
            pltpu.VMEM((2, 2, fields, ny, nz), f32),
            pltpu.VMEM((2,) + plane, f32),
            pltpu.VMEM((2,) + plane, f32),
            pltpu.VMEM(plane, f32),
            pltpu.VMEM(plane, f32),
            pltpu.VMEM(plane, f32),
            dma((steps,)),
            dma((steps,)),
            dma((2, 2, groups)),
            dma((2, 2, groups)),
            dma((2, nx)),
            dma((2, nx)),
            dma((nx,)),
            dma((nx,)),
        ],
        compiler_params=pltpu.CompilerParams(
            collective_id=0, has_side_effects=True, vmem_limit_bytes=40 * 2**20),
    )(primal, source, guess, mixing)


def solution(mesh):
    placed = P("tm", None, "space", None, None)
    return jax.shard_map(
        functools.partial(per_device, mesh.shape["tm"], mesh.shape["space"]),
        mesh=mesh,
        in_specs=(placed, placed, placed, P()),
        out_specs=(placed, placed),
        check_vma=False,
    )
```

```python
import functools

import jax
import jax.numpy as jnp
from jax import lax
from jax.experimental import pallas as pl
from jax.experimental.pallas import tpu as pltpu
from jax.sharding import PartitionSpec as P

DIFFUSION = 0.1
RATE = 0.25
COARSE_STEP = 0.75
KEEP = 1.0 - 6.0 * DIFFUSION - RATE
MESH = pl.DeviceIdType.MESH
LEFT, RIGHT = 0, 1
PAD = 8


def kernel(blocks, slabs, primal_hbm, source_hbm, guess_hbm, mixing, fine_hbm, residual_hbm,
           primal, source, guess, fine, residual_out, scaled, state, halo, ends, end_in, relaxed, moved, moved_in,
           load_p, load_s, load_g, store_f, store_r, halo_send, halo_recv, end_send, end_recv, err_send, err_recv):
    steps, fields, nx, ny, nz = primal.shape
    last = nx - 1
    position = lax.axis_index("tm")
    slab = lax.axis_index("space")
    side = {LEFT: lax.rem(slab + slabs - 1, slabs), RIGHT: lax.rem(slab + 1, slabs)}
    edge = {LEFT: 0, RIGHT: last}
    first_block = position == 0
    has_next = position < blocks - 1
    groups = halo_send.shape[-1]
    cuts = [(g * fields) // groups for g in range(groups + 1)]

    def load_primal(t):
        return pltpu.make_async_copy(primal_hbm.at[t], primal.at[t], load_p.at[t])

    def load_source(t):
        return pltpu.make_async_copy(source_hbm.at[t], source.at[t], load_s.at[t])

    def store_fine(t):
        return pltpu.make_async_copy(fine.at[t], fine_hbm.at[t], store_f.at[t])

    load_guess = pltpu.make_async_copy(guess_hbm, guess, load_g)
    store_residual = pltpu.make_async_copy(residual_out, residual_hbm, store_r)
    load_guess.start()
    load_primal(0).start()
    load_source(0).start()
    for t in range(1, steps):
        load_source(t).start()
        load_primal(t).start()

    barrier = pltpu.get_barrier_semaphore()
    for way in (LEFT, RIGHT):
        pl.semaphore_signal(barrier, inc=1, device_id={"space": side[way]}, device_id_type=MESH)

    @pl.when(has_next)
    def _():
        pl.semaphore_signal(barrier, inc=1, device_id={"tm": position + 1}, device_id_type=MESH)

    @pl.when(jnp.logical_not(first_block))
    def _():
        pl.semaphore_signal(barrier, inc=1, device_id={"tm": position - 1}, device_id_type=MESH)

    pl.semaphore_wait(barrier, 2 + jnp.where(first_block, 0, 1) + jnp.where(has_next, 1, 0))

    weights = [[mixing[i, j] for j in range(fields)] for i in range(fields)]

    def mix(values, i):
        total = weights[i][0] * values[0]
        for j in range(1, fields):
            total = total + weights[i][j] * values[j]
        return total

    body = pl.ds(PAD, ny)
    blank = jnp.zeros((PAD, nz), jnp.float32)

    def clear(x, carry):
        for slot in range(2):
            for f in range(fields):
                state[slot, x, f, pl.ds(0, PAD)] = blank
                state[slot, x, f, pl.ds(PAD + ny, PAD)] = blank
        return carry

    lax.fori_loop(0, nx, clear, 0)

    def halo_copy(way, slot, g):
        part = pl.ds(cuts[g], cuts[g + 1] - cuts[g])
        return pltpu.make_async_remote_copy(
            src_ref=state.at[slot, edge[way], part, body],
            dst_ref=halo.at[way, slot, part],
            send_sem=halo_send.at[way, slot, g],
            recv_sem=halo_recv.at[way, slot, g],
            device_id={"space": side[way]},
            device_id_type=MESH,
        )

    def end_copy(m, x):
        return pltpu.make_async_remote_copy(
            src_ref=ends.at[m, x], dst_ref=end_in.at[m, x],
            send_sem=end_send.at[m, x], recv_sem=end_recv.at[m, x],
            device_id={"tm": position + 1}, device_id_type=MESH,
        )

    def err_copy(x):
        return pltpu.make_async_remote_copy(
            src_ref=moved.at[x], dst_ref=moved_in.at[x],
            send_sem=err_send.at[x], recv_sem=err_recv.at[x],
            device_id={"tm": position + 1}, device_id_type=MESH,
        )

    def stepped(slot, t, x, near):
        values = [state[slot, x, f, body] for f in range(fields)]
        results = []
        for f in range(fields):
            v = values[f]
            around = pltpu.roll(v, 1, 1) + pltpu.roll(v, nz - 1, 1)
            around = around + state[slot, x, f, pl.ds(PAD - 1, ny)]
            around = around + state[slot, x, f, pl.ds(PAD + 1, ny)]
            for other in near:
                around = around + state[slot, other, f, body]
            results.append(KEEP * v + DIFFUSION * around + scaled[t, f, x] * mix(values, f))
        return results

    def step(m, slot, t, ways, closing):
        final = m == 2

        def given(x, f, value):
            return value if closing and not final else value + source[t + 1, f, x]

        def put(x, f, value):
            if closing and not final:
                ends[m, x, f] = value
                return
            if final:
                fine[t + 1, f, x] = value
            if not closing:
                state[1 - slot, x, f, body] = value

        if m == 0:
            load_primal(t).wait()
            if not closing:
                load_source(t + 1).wait()

            def slope(x, carry):
                values = [primal[t, f, x] for f in range(fields)]
                for f in range(fields):
                    bent = jnp.tanh(mix(values, f))
                    scaled[t, f, x] = RATE - RATE * (bent * bent)
                return carry

            lax.fori_loop(0, nx, slope, 0, unroll=2)

        def inner(x, carry):
            results = stepped(slot, t, x, (x - 1, x + 1))
            for f in range(fields):
                put(x, f, given(x, f, results[f]))
            if closing and not final:
                @pl.when(has_next)
                def _():
                    end_copy(m, x).start()
            return carry

        for x in range(1, last):
            inner(x, 0)
        waiting = []
        for way in ways:
            target = RIGHT if way == LEFT else LEFT
            x = edge[target]
            results = stepped(slot, t, x, (x + 1 if target == LEFT else x - 1,))
            waiting.append((way, target, x, [given(x, f, results[f]) for f in range(fields)]))
        for way, target, x, results in waiting:
            for g in range(groups):
                halo_copy(way, slot, g).wait_recv()
                for f in range(cuts[g], cuts[g + 1]):
                    put(x, f, results[f] + DIFFUSION * halo[way, slot, f])
                if not closing:
                    halo_copy(target, 1 - slot, g).start()
            if closing and not final:
                @pl.when(has_next)
                def _():
                    end_copy(m, x).start()
        for way in ways:
            for g in range(groups):
                halo_copy(way, slot, g).wait_send()
        if final:
            store_fine(t + 1).start()

    forward, backward = (LEFT, RIGHT), (RIGHT, LEFT)

    def march(m, count):
        pairs = (count - 1) // 2

        def pair(i, carry):
            step(m, 0, 2 * i, forward, False)
            step(m, 1, 2 * i + 1, backward, False)
            return carry

        lax.fori_loop(0, pairs, pair, 0)
        for t in range(2 * pairs, count):
            step(m, t % 2, t, (forward, backward)[t % 2], t == count - 1)

    def send_edge(way):
        for g in range(groups):
            halo_copy(way, 0, g).start()

    def begin(place):
        place(edge[LEFT])
        send_edge(LEFT)
        place(edge[RIGHT])
        send_edge(RIGHT)

        def rest(x, carry):
            place(x)
            return carry

        lax.fori_loop(1, last, rest, 0)

    def from_guess(x):
        for f in range(fields):
            state[0, x, f, body] = guess[0, f, x]

    load_guess.wait()
    begin(from_guess)
    load_source(0).wait()
    march(0, steps)

    def from_end(x):
        @pl.when(first_block)
        def _():
            for f in range(fields):
                value = guess[0, f, x]
                state[0, x, f, body] = value
                relaxed[x, f] = value

        @pl.when(jnp.logical_not(first_block))
        def _():
            end_copy(0, x).wait_recv()
            for f in range(fields):
                value = end_in[0, x, f] + source[0, f, x]
                state[0, x, f, body] = value
                relaxed[x, f] = value

    begin(from_end)
    march(1, steps)

    def from_error(x):
        @pl.when(first_block)
        def _():
            for f in range(fields):
                value = source[0, f, x]
                residual_out[0, f, x] = value
                moved_in[x, f] = value

        @pl.when(jnp.logical_not(first_block))
        def _():
            end_copy(1, x).wait_recv()
            rest = []
            for f in range(fields):
                value = end_in[1, x, f] + source[0, f, x] - relaxed[x, f]
                residual_out[0, f, x] = value
                rest.append(value)
            err_copy(x).wait_recv()
            for f in range(fields):
                moved_in[x, f] = moved_in[x, f] + rest[f]

        error = [moved_in[x, f] for f in range(fields)]

        @pl.when(has_next)
        def _():
            for f in range(fields):
                moved[x, f] = (1.0 - COARSE_STEP) * error[f] + (COARSE_STEP / RATE) * (
                    scaled[0, f, x] * mix(error, f))
            err_copy(x).start()

        for f in range(fields):
            value = relaxed[x, f] + error[f]
            state[0, x, f, body] = value
            fine[0, f, x] = value

    begin(from_error)
    store_fine(0).start()
    store_residual.start()
    march(2, steps - 1)
    for t in range(steps):
        store_fine(t).wait()
    store_residual.wait()

    @pl.when(has_next)
    def _():
        def drain(x, carry):
            end_copy(0, x).wait_send()
            end_copy(1, x).wait_send()
            err_copy(x).wait_send()
            return carry

        lax.fori_loop(0, nx, drain, 0)


def per_device(blocks, slabs, primal, source, guess, mixing):
    steps, fields, nx, ny, nz = primal.shape
    groups = 2
    plane = (nx, fields, ny, nz)
    padded = (nx, fields, ny + 2 * PAD, nz)
    anywhere = pl.BlockSpec(memory_space=pl.ANY)
    dma = pltpu.SemaphoreType.DMA
    f32 = jnp.float32
    return pl.pallas_call(
        functools.partial(kernel, blocks, slabs),
        out_shape=(jax.ShapeDtypeStruct(primal.shape, f32), jax.ShapeDtypeStruct(guess.shape, f32)),
        in_specs=[anywhere] * 3 + [pl.BlockSpec(memory_space=pltpu.SMEM)],
        out_specs=(anywhere, anywhere),
        scratch_shapes=[
            pltpu.VMEM(primal.shape, f32),
            pltpu.VMEM(primal.shape, f32),
            pltpu.VMEM(guess.shape, f32),
            pltpu.VMEM(primal.shape, f32),
            pltpu.VMEM(guess.shape, f32),
            pltpu.VMEM(primal.shape, f32),
            pltpu.VMEM((2,) + padded, f32),
            pltpu.VMEM((2, 2, fields, ny, nz), f32),
            pltpu.VMEM((2,) + plane, f32),
            pltpu.VMEM((2,) + plane, f32),
            pltpu.VMEM(plane, f32),
            pltpu.VMEM(plane, f32),
            pltpu.VMEM(plane, f32),
            dma((steps,)),
            dma((steps,)),
            dma,
            dma((steps,)),
            dma,
            dma((2, 2, groups)),
            dma((2, 2, groups)),
            dma((2, nx)),
            dma((2, nx)),
            dma((nx,)),
            dma((nx,)),
        ],
        compiler_params=pltpu.CompilerParams(
            collective_id=0, has_side_effects=True, vmem_limit_bytes=60 * 2**20),
    )(primal, source, guess, mixing)


def solution(mesh):
    placed = P("tm", None, "space", None, None)
    return jax.shard_map(
        functools.partial(per_device, mesh.shape["tm"], mesh.shape["space"]),
        mesh=mesh,
        in_specs=(placed, placed, placed, P()),
        out_specs=(placed, placed),
        check_vma=False,
    )
```

```python
import functools

import jax
import jax.numpy as jnp
from jax import lax
from jax.experimental import pallas as pl
from jax.experimental.pallas import tpu as pltpu
from jax.sharding import PartitionSpec as P

DIFFUSION = 0.1
RATE = 0.25
COARSE_STEP = 0.75
KEEP = 1.0 - 6.0 * DIFFUSION - RATE
MESH = pl.DeviceIdType.MESH
LEFT, RIGHT = 0, 1
PAD = 8


def kernel(blocks, slabs, team, primal_hbm, source_hbm, guess_hbm, mixing, fine, residual_out,
           primal, source, guess, scaled, state, halo, ends, end_in, relaxed, moved, moved_in,
           slabs_in, far_in, far_out,
           load_p, load_s, load_g, halo_send, halo_recv, end_send, end_recv, err_send, err_recv,
           slab_send, slab_recv, far_send, far_recv, tree_send):
    steps, fields, nx, ny, nz = primal.shape
    last = nx - 1
    position = lax.axis_index("tm")
    slab = lax.axis_index("space")
    side = {LEFT: lax.rem(slab + slabs - 1, slabs), RIGHT: lax.rem(slab + 1, slabs)}
    edge = {LEFT: 0, RIGHT: last}
    first_block = position == 0
    has_next = position < blocks - 1
    member = lax.rem(position, team)
    closes_team = member == team - 1
    first_team = position < team
    last_team = position >= blocks - team
    depth = team.bit_length() - 1

    def is_parent(b):
        return lax.rem(position, 2 << b) == (2 << b) - 1

    def is_child(b):
        return lax.rem(position, 2 << b) == (1 << b) - 1
    groups = halo_send.shape[-1]
    cuts = [(g * fields) // groups for g in range(groups + 1)]

    def load_primal(t):
        return pltpu.make_async_copy(primal_hbm.at[t], primal.at[t], load_p.at[t])

    def load_source(t):
        return pltpu.make_async_copy(source_hbm.at[t], source.at[t], load_s.at[t])

    load_guess = pltpu.make_async_copy(guess_hbm, guess, load_g)
    load_guess.start()
    load_primal(0).start()
    load_source(0).start()
    for t in range(1, steps):
        load_source(t).start()
        load_primal(t).start()

    barrier = pltpu.get_barrier_semaphore()
    for way in (LEFT, RIGHT):
        pl.semaphore_signal(barrier, inc=1, device_id={"space": side[way]}, device_id_type=MESH)

    peers = [
        (jnp.logical_not(first_block), -1),
        (has_next, 1),
        (jnp.logical_and(closes_team, jnp.logical_not(first_team)), -team),
        (jnp.logical_and(closes_team, jnp.logical_not(last_team)), team),
    ]
    for b in range(depth):
        peers += [(is_parent(b), -(1 << b)), (is_child(b), 1 << b)]
    expected = 2
    for met, offset in peers:
        expected = expected + jnp.where(met, 1, 0)

        @pl.when(met)
        def _():
            pl.semaphore_signal(
                barrier, inc=1, device_id={"tm": position + offset}, device_id_type=MESH)

    pl.semaphore_wait(barrier, expected)

    weights = [[mixing[i, j] for j in range(fields)] for i in range(fields)]

    def mix(values, i):
        total = weights[i][0] * values[0]
        for j in range(1, fields):
            total = total + weights[i][j] * values[j]
        return total

    body = pl.ds(PAD, ny)
    blank = jnp.zeros((PAD, nz), jnp.float32)

    def clear(x, carry):
        for slot in range(2):
            for f in range(fields):
                state[slot, x, f, pl.ds(0, PAD)] = blank
                state[slot, x, f, pl.ds(PAD + ny, PAD)] = blank
        return carry

    lax.fori_loop(0, nx, clear, 0)

    def halo_copy(way, slot, g):
        part = pl.ds(cuts[g], cuts[g + 1] - cuts[g])
        return pltpu.make_async_remote_copy(
            src_ref=state.at[slot, edge[way], part, body],
            dst_ref=halo.at[way, slot, part],
            send_sem=halo_send.at[way, slot, g],
            recv_sem=halo_recv.at[way, slot, g],
            device_id={"space": side[way]},
            device_id_type=MESH,
        )

    def end_copy(m, x):
        return pltpu.make_async_remote_copy(
            src_ref=ends.at[m, x], dst_ref=end_in.at[m, x],
            send_sem=end_send.at[m, x], recv_sem=end_recv.at[m, x],
            device_id={"tm": position + 1}, device_id_type=MESH,
        )

    def err_copy(x):
        return pltpu.make_async_remote_copy(
            src_ref=moved.at[x], dst_ref=moved_in.at[x],
            send_sem=err_send.at[x], recv_sem=err_recv.at[x],
            device_id={"tm": position + 1}, device_id_type=MESH,
        )

    def slab_copy(src, j):
        return pltpu.make_async_remote_copy(
            src_ref=src, dst_ref=slabs_in.at[j],
            send_sem=slab_send.at[j], recv_sem=slab_recv.at[j],
            device_id={"tm": position + 1}, device_id_type=MESH,
        )

    def far_copy(x):
        return pltpu.make_async_remote_copy(
            src_ref=far_out.at[x], dst_ref=far_in.at[x],
            send_sem=far_send.at[x], recv_sem=far_recv.at[x],
            device_id={"tm": position + team}, device_id_type=MESH,
        )

    def tree_copy(b, x):
        return pltpu.make_async_remote_copy(
            src_ref=far_in.at[x], dst_ref=far_in.at[x],
            send_sem=tree_send.at[b, x], recv_sem=far_recv.at[x],
            device_id={"tm": position - (1 << b)}, device_id_type=MESH,
        )

    def send_slab():
        @pl.when(jnp.logical_not(closes_team))
        def _():
            slab_copy(scaled.at[0], member).start()

    def pass_slab(hop):
        @pl.when(member >= hop)
        def _():
            j = member - hop
            slab_copy(slabs_in.at[j], j).wait_recv()

            @pl.when(jnp.logical_not(closes_team))
            def _():
                slab_copy(slabs_in.at[j], j).start()

    def slopes(t):
        load_primal(t).wait()

        def slope(x, carry):
            values = [primal[t, f, x] for f in range(fields)]
            for f in range(fields):
                bent = jnp.tanh(mix(values, f))
                scaled[t, f, x] = RATE - RATE * (bent * bent)
            return carry

        lax.fori_loop(0, nx, slope, 0, unroll=2)

    def coarse(slope, values):
        return [(1.0 - COARSE_STEP) * values[f]
                + (COARSE_STEP / RATE) * (slope[f] * mix(values, f)) for f in range(fields)]

    def stepped(slot, t, x, near):
        values = [state[slot, x, f, body] for f in range(fields)]
        results = []
        for f in range(fields):
            v = values[f]
            around = pltpu.roll(v, 1, 1) + pltpu.roll(v, nz - 1, 1)
            around = around + state[slot, x, f, pl.ds(PAD - 1, ny)]
            around = around + state[slot, x, f, pl.ds(PAD + 1, ny)]
            for other in near:
                around = around + state[slot, other, f, body]
            results.append(KEEP * v + DIFFUSION * around + scaled[t, f, x] * mix(values, f))
        return results

    early = (1, last - 1)

    def step(m, slot, t, ways, closing):
        final = m == 2

        def given(x, f, value):
            return value if closing and not final else value + source[t + 1, f, x]

        def put(x, f, value):
            if closing and not final:
                ends[m, x, f] = value
                return
            if final:
                fine[t + 1, f, x] = value
            if not closing:
                state[1 - slot, x, f, body] = value

        if m == 0 and not closing:
            load_source(t + 1).wait()
            slopes(t + 1)

        def inner(x):
            results = stepped(slot, t, x, (x - 1, x + 1))
            for f in range(fields):
                put(x, f, given(x, f, results[f]))

        for x in range(1, last):
            inner(x)
            if closing and not final and x in early:
                @pl.when(has_next)
                def _():
                    end_copy(m, x).start()
        waiting = []
        for way in ways:
            target = RIGHT if way == LEFT else LEFT
            x = edge[target]
            results = stepped(slot, t, x, (x + 1 if target == LEFT else x - 1,))
            waiting.append((way, target, x, [given(x, f, results[f]) for f in range(fields)]))
        for way, target, x, results in waiting:
            for g in range(groups):
                halo_copy(way, slot, g).wait_recv()
                for f in range(cuts[g], cuts[g + 1]):
                    put(x, f, results[f] + DIFFUSION * halo[way, slot, f])
                if not closing:
                    halo_copy(target, 1 - slot, g).start()
            if closing and not final:
                @pl.when(has_next)
                def _():
                    end_copy(m, x).start()
        if closing and not final:
            @pl.when(has_next)
            def _():
                for x in range(1, last):
                    if x not in early:
                        end_copy(m, x).start()
        for way in ways:
            for g in range(groups):
                halo_copy(way, slot, g).wait_send()

    forward, backward = (LEFT, RIGHT), (RIGHT, LEFT)

    def march(m, count, between=()):
        pairs = (count - 1) // 2

        def pair(i, carry):
            step(m, 0, 2 * i, forward, False)
            step(m, 1, 2 * i + 1, backward, False)
            return carry

        lax.fori_loop(0, pairs, pair, 0)
        for hop in between:
            pass_slab(hop)
        for t in range(2 * pairs, count):
            step(m, t % 2, t, (forward, backward)[t % 2], t == count - 1)

    def send_edge(way):
        for g in range(groups):
            halo_copy(way, 0, g).start()

    def begin(place):
        place(edge[LEFT])
        send_edge(LEFT)
        place(edge[RIGHT])
        send_edge(RIGHT)

        def rest(x, carry):
            place(x)
            return carry

        lax.fori_loop(1, last, rest, 0)

    def from_guess(x):
        for f in range(fields):
            state[0, x, f, body] = guess[0, f, x]

    load_guess.wait()
    begin(from_guess)
    slopes(0)
    send_slab()
    load_source(0).wait()
    march(0, steps, (1,) if team > 2 else ())

    def from_end(x):
        @pl.when(first_block)
        def _():
            for f in range(fields):
                value = guess[0, f, x]
                state[0, x, f, body] = value
                relaxed[x, f] = value

        @pl.when(jnp.logical_not(first_block))
        def _():
            end_copy(0, x).wait_recv()
            for f in range(fields):
                value = end_in[0, x, f] + source[0, f, x]
                state[0, x, f, body] = value
                relaxed[x, f] = value

    begin(from_end)
    march(1, steps, range(2, team - 1))

    def last_slab():
        @pl.when(closes_team)
        def _():
            slab_copy(slabs_in.at[0], 0).wait_recv()

    def near(x):
        @pl.when(first_block)
        def _():
            for f in range(fields):
                value = source[0, f, x]
                residual_out[0, f, x] = value
                moved_in[x, f] = value

        @pl.when(jnp.logical_not(first_block))
        def _():
            end_copy(1, x).wait_recv()
            rest = []
            for f in range(fields):
                value = end_in[1, x, f] + source[0, f, x] - relaxed[x, f]
                residual_out[0, f, x] = value
                rest.append(value)

            @pl.when(member == 0)
            def _():
                for f in range(fields):
                    moved_in[x, f] = rest[f]

            @pl.when(member > 0)
            def _():
                err_copy(x).wait_recv()
                for f in range(fields):
                    moved_in[x, f] = moved_in[x, f] + rest[f]

        @pl.when(jnp.logical_not(closes_team))
        def _():
            error = coarse([scaled[0, f, x] for f in range(fields)],
                           [moved_in[x, f] for f in range(fields)])
            for f in range(fields):
                moved[x, f] = error[f]
            err_copy(x).start()

    def from_error(x):
        @pl.when(closes_team)
        def _():
            near(x)

        @pl.when(jnp.logical_not(first_team))
        def _():
            far_copy(x).wait_recv()

            def through(j, values):
                return tuple(coarse([slabs_in[j, f, x] for f in range(fields)], list(values)))

            values = lax.fori_loop(
                0, member, through, tuple(far_in[x, f] for f in range(fields)))
            for f in range(fields):
                moved_in[x, f] = moved_in[x, f] + values[f]

        error = [moved_in[x, f] for f in range(fields)]

        @pl.when(jnp.logical_and(closes_team, jnp.logical_not(last_team)))
        def _():
            going = coarse([scaled[0, f, x] for f in range(fields)], error)
            for f in range(fields):
                far_out[x, f] = going[f]
            far_copy(x).start()

        for b in reversed(range(depth)):
            @pl.when(jnp.logical_and(is_parent(b), jnp.logical_not(first_team)))
            def _():
                tree_copy(b, x).start()

        for f in range(fields):
            value = relaxed[x, f] + error[f]
            state[0, x, f, body] = value
            fine[0, f, x] = value

    last_slab()

    @pl.when(jnp.logical_not(closes_team))
    def _():
        near(0)
        near(last)

        def rest(x, carry):
            near(x)
            return carry

        lax.fori_loop(1, last, rest, 0)

    begin(from_error)
    march(2, steps - 1)

    def drain(x, carry):
        @pl.when(has_next)
        def _():
            end_copy(0, x).wait_send()
            end_copy(1, x).wait_send()

        @pl.when(jnp.logical_not(closes_team))
        def _():
            err_copy(x).wait_send()

        @pl.when(jnp.logical_and(closes_team, jnp.logical_not(last_team)))
        def _():
            far_copy(x).wait_send()

        for b in range(depth):
            @pl.when(jnp.logical_and(is_parent(b), jnp.logical_not(first_team)))
            def _():
                tree_copy(b, x).wait_send()
        return carry

    lax.fori_loop(0, nx, drain, 0)

    @pl.when(jnp.logical_not(closes_team))
    def _():
        def drain_slab(j, carry):
            slab_copy(slabs_in.at[j], j).wait_send()
            return carry

        lax.fori_loop(0, member, drain_slab, 0)
        slab_copy(scaled.at[0], member).wait_send()


def per_device(blocks, slabs, primal, source, guess, mixing):
    steps, fields, nx, ny, nz = primal.shape
    groups = 2
    plane = (nx, fields, ny, nz)
    padded = (nx, fields, ny + 2 * PAD, nz)
    hbm = pl.BlockSpec(memory_space=pltpu.HBM)
    vmem = pl.BlockSpec(memory_space=pltpu.VMEM)
    team = 2
    while (2 * team) ** 2 <= blocks and blocks % (2 * team) == 0:
        team *= 2
    dma = pltpu.SemaphoreType.DMA
    f32 = jnp.float32
    return pl.pallas_call(
        functools.partial(kernel, blocks, slabs, team),
        out_shape=(jax.ShapeDtypeStruct(primal.shape, f32), jax.ShapeDtypeStruct(guess.shape, f32)),
        in_specs=[hbm] * 3 + [pl.BlockSpec(memory_space=pltpu.SMEM)],
        out_specs=(vmem, vmem),
        scratch_shapes=[
            pltpu.VMEM(primal.shape, f32),
            pltpu.VMEM(primal.shape, f32),
            pltpu.VMEM(guess.shape, f32),
            pltpu.VMEM(primal.shape, f32),
            pltpu.VMEM((2,) + padded, f32),
            pltpu.VMEM((2, 2, fields, ny, nz), f32),
            pltpu.VMEM((2,) + plane, f32),
            pltpu.VMEM((2,) + plane, f32),
            pltpu.VMEM(plane, f32),
            pltpu.VMEM(plane, f32),
            pltpu.VMEM(plane, f32),
            pltpu.VMEM((team - 1,) + primal.shape[1:], f32),
            pltpu.VMEM(plane, f32),
            pltpu.VMEM(plane, f32),
            dma((steps,)),
            dma((steps,)),
            dma,
            dma((2, 2, groups)),
            dma((2, 2, groups)),
            dma((2, nx)),
            dma((2, nx)),
            dma((nx,)),
            dma((nx,)),
            dma((team,)),
            dma((team,)),
            dma((nx,)),
            dma((nx,)),
            dma((team.bit_length() - 1, nx)),
        ],
        compiler_params=pltpu.CompilerParams(
            collective_id=0, has_side_effects=True, vmem_limit_bytes=48 * 2**20),
    )(primal, source, guess, mixing)


def solution(mesh):
    placed = P("tm", None, "space", None, None)
    return jax.shard_map(
        functools.partial(per_device, mesh.shape["tm"], mesh.shape["space"]),
        mesh=mesh,
        in_specs=(placed, placed, placed, P()),
        out_specs=(placed, placed),
        check_vma=False,
    )
```

```python
import functools

import jax
import jax.numpy as jnp
from jax import lax
from jax.experimental import pallas as pl
from jax.experimental.pallas import tpu as pltpu
from jax.sharding import PartitionSpec as P

DIFFUSION = 0.1
RATE = 0.25
COARSE_STEP = 0.75
KEEP = 1.0 - 6.0 * DIFFUSION - RATE
MESH = pl.DeviceIdType.MESH
LEFT, RIGHT = 0, 1
PAD = 8


def kernel(blocks, slabs, team, primal_hbm, source_hbm, guess_hbm, mixing, fine_hbm, residual_hbm,
           primal, source, guess, fine, residual_out, scaled, state, halo, ends, end_in, relaxed, moved, moved_in,
           slabs_in, far_in, far_out,
           load_p, load_s, load_g, store_f, store_r, halo_send, halo_recv, end_send, end_recv, err_send, err_recv,
           slab_send, slab_recv, far_send, far_recv, tree_send):
    steps, fields, nx, ny, nz = primal.shape
    last = nx - 1
    position = lax.axis_index("tm")
    slab = lax.axis_index("space")
    side = {LEFT: lax.rem(slab + slabs - 1, slabs), RIGHT: lax.rem(slab + 1, slabs)}
    edge = {LEFT: 0, RIGHT: last}
    first_block = position == 0
    has_next = position < blocks - 1
    member = lax.rem(position, team)
    closes_team = member == team - 1
    first_team = position < team
    last_team = position >= blocks - team
    depth = team.bit_length() - 1

    def is_parent(b):
        return lax.rem(position, 2 << b) == (2 << b) - 1

    def is_child(b):
        return lax.rem(position, 2 << b) == (1 << b) - 1
    groups = halo_send.shape[-1]
    cuts = [(g * fields) // groups for g in range(groups + 1)]

    def load_primal(t):
        return pltpu.make_async_copy(primal_hbm.at[t], primal.at[t], load_p.at[t])

    def load_source(t):
        return pltpu.make_async_copy(source_hbm.at[t], source.at[t], load_s.at[t])

    def store_fine(t):
        return pltpu.make_async_copy(fine.at[t], fine_hbm.at[t], store_f.at[t])

    store_residual = pltpu.make_async_copy(residual_out, residual_hbm, store_r)
    load_guess = pltpu.make_async_copy(guess_hbm, guess, load_g)
    load_guess.start()
    load_primal(0).start()
    load_source(0).start()
    for t in range(1, steps):
        load_source(t).start()
        load_primal(t).start()

    barrier = pltpu.get_barrier_semaphore()
    for way in (LEFT, RIGHT):
        pl.semaphore_signal(barrier, inc=1, device_id={"space": side[way]}, device_id_type=MESH)

    peers = [
        (jnp.logical_not(first_block), -1),
        (has_next, 1),
        (jnp.logical_and(closes_team, jnp.logical_not(first_team)), -team),
        (jnp.logical_and(closes_team, jnp.logical_not(last_team)), team),
    ]
    for b in range(depth):
        peers += [(is_parent(b), -(1 << b)), (is_child(b), 1 << b)]
    expected = 2
    for met, offset in peers:
        expected = expected + jnp.where(met, 1, 0)

        @pl.when(met)
        def _():
            pl.semaphore_signal(
                barrier, inc=1, device_id={"tm": position + offset}, device_id_type=MESH)

    pl.semaphore_wait(barrier, expected)

    weights = [[mixing[i, j] for j in range(fields)] for i in range(fields)]

    def mix(values, i):
        total = weights[i][0] * values[0]
        for j in range(1, fields):
            total = total + weights[i][j] * values[j]
        return total

    body = pl.ds(PAD, ny)
    blank = jnp.zeros((PAD, nz), jnp.float32)

    def clear(x, carry):
        for slot in range(2):
            for f in range(fields):
                state[slot, x, f, pl.ds(0, PAD)] = blank
                state[slot, x, f, pl.ds(PAD + ny, PAD)] = blank
        return carry

    lax.fori_loop(0, nx, clear, 0)

    def halo_copy(way, slot, g, given=False):
        part = pl.ds(cuts[g], cuts[g + 1] - cuts[g])
        return pltpu.make_async_remote_copy(
            src_ref=guess_hbm.at[0, part, edge[way]] if given
            else state.at[slot, edge[way], part, body],
            dst_ref=halo.at[way, slot, part],
            send_sem=halo_send.at[way, slot, g],
            recv_sem=halo_recv.at[way, slot, g],
            device_id={"space": side[way]},
            device_id_type=MESH,
        )

    def end_copy(m, x):
        return pltpu.make_async_remote_copy(
            src_ref=ends.at[m, x], dst_ref=end_in.at[m, x],
            send_sem=end_send.at[m, x], recv_sem=end_recv.at[m, x],
            device_id={"tm": position + 1}, device_id_type=MESH,
        )

    def err_copy(x):
        return pltpu.make_async_remote_copy(
            src_ref=moved.at[x], dst_ref=moved_in.at[x],
            send_sem=err_send.at[x], recv_sem=err_recv.at[x],
            device_id={"tm": position + 1}, device_id_type=MESH,
        )

    def slab_copy(src, j):
        return pltpu.make_async_remote_copy(
            src_ref=src, dst_ref=slabs_in.at[j],
            send_sem=slab_send.at[j], recv_sem=slab_recv.at[j],
            device_id={"tm": position + 1}, device_id_type=MESH,
        )

    def far_copy(x):
        return pltpu.make_async_remote_copy(
            src_ref=far_out.at[x], dst_ref=far_in.at[x],
            send_sem=far_send.at[x], recv_sem=far_recv.at[x],
            device_id={"tm": position + team}, device_id_type=MESH,
        )

    def tree_copy(b, x):
        return pltpu.make_async_remote_copy(
            src_ref=far_in.at[x], dst_ref=far_in.at[x],
            send_sem=tree_send.at[b, x], recv_sem=far_recv.at[x],
            device_id={"tm": position - (1 << b)}, device_id_type=MESH,
        )

    def send_slab():
        @pl.when(jnp.logical_not(closes_team))
        def _():
            slab_copy(scaled.at[0], member).start()

    def pass_slab(hop):
        @pl.when(member >= hop)
        def _():
            j = member - hop
            slab_copy(slabs_in.at[j], j).wait_recv()

            @pl.when(jnp.logical_not(closes_team))
            def _():
                slab_copy(slabs_in.at[j], j).start()

    def slopes(t):
        load_primal(t).wait()

        def slope(x, carry):
            values = [primal[t, f, x] for f in range(fields)]
            for f in range(fields):
                bent = jnp.tanh(mix(values, f))
                scaled[t, f, x] = RATE - RATE * (bent * bent)
            return carry

        lax.fori_loop(0, nx, slope, 0, unroll=2)

    def coarse(slope, values):
        return [(1.0 - COARSE_STEP) * values[f]
                + (COARSE_STEP / RATE) * (slope[f] * mix(values, f)) for f in range(fields)]

    def stepped(slot, t, x, near):
        values = [state[slot, x, f, body] for f in range(fields)]
        results = []
        for f in range(fields):
            v = values[f]
            around = pltpu.roll(v, 1, 1) + pltpu.roll(v, nz - 1, 1)
            around = around + state[slot, x, f, pl.ds(PAD - 1, ny)]
            around = around + state[slot, x, f, pl.ds(PAD + 1, ny)]
            for other in near:
                around = around + state[slot, other, f, body]
            results.append(KEEP * v + DIFFUSION * around + scaled[t, f, x] * mix(values, f))
        return results

    early = (1, last - 1)

    def step(m, slot, t, ways, closing):
        final = m == 2

        def given(x, f, value):
            return value if closing and not final else value + source[t + 1, f, x]

        def put(x, f, value):
            if closing and not final:
                ends[m, x, f] = value
                return
            if final:
                fine[t + 1, f, x] = value
            if not closing:
                state[1 - slot, x, f, body] = value

        if m == 0 and not closing:
            load_source(t + 1).wait()
            slopes(t + 1)

        def inner(x):
            results = stepped(slot, t, x, (x - 1, x + 1))
            for f in range(fields):
                put(x, f, given(x, f, results[f]))

        for x in range(1, last):
            inner(x)
            if closing and not final and x in early:
                @pl.when(has_next)
                def _():
                    end_copy(m, x).start()
        waiting = []
        for way in ways:
            target = RIGHT if way == LEFT else LEFT
            x = edge[target]
            results = stepped(slot, t, x, (x + 1 if target == LEFT else x - 1,))
            waiting.append((way, target, x, [given(x, f, results[f]) for f in range(fields)]))
        for way, target, x, results in waiting:
            for g in range(groups):
                halo_copy(way, slot, g).wait_recv()
                for f in range(cuts[g], cuts[g + 1]):
                    put(x, f, results[f] + DIFFUSION * halo[way, slot, f])
                if not closing:
                    halo_copy(target, 1 - slot, g).start()
            if closing and not final:
                @pl.when(has_next)
                def _():
                    end_copy(m, x).start()
        if closing and not final:
            @pl.when(has_next)
            def _():
                for x in range(1, last):
                    if x not in early:
                        end_copy(m, x).start()
        for way in ways:
            for g in range(groups):
                halo_copy(way, slot, g).wait_send()
        if final:
            store_fine(t + 1).start()

    forward, backward = (LEFT, RIGHT), (RIGHT, LEFT)

    def march(m, count, between=()):
        pairs = (count - 1) // 2

        def pair(i, carry):
            step(m, 0, 2 * i, forward, False)
            step(m, 1, 2 * i + 1, backward, False)
            return carry

        lax.fori_loop(0, pairs, pair, 0)
        for hop in between:
            pass_slab(hop)
        for t in range(2 * pairs, count):
            step(m, t % 2, t, (forward, backward)[t % 2], t == count - 1)

    def send_edge(way):
        for g in range(groups):
            halo_copy(way, 0, g).start()

    def begin(place):
        place(edge[LEFT])
        send_edge(LEFT)
        place(edge[RIGHT])
        send_edge(RIGHT)

        def rest(x, carry):
            place(x)
            return carry

        lax.fori_loop(1, last, rest, 0)

    def from_guess(x):
        for f in range(fields):
            state[0, x, f, body] = guess[0, f, x]

    for way in (LEFT, RIGHT):
        for g in range(groups):
            halo_copy(way, 0, g, True).start()
    load_guess.wait()

    def copy_guess(x, carry):
        from_guess(x)
        return carry

    lax.fori_loop(0, nx, copy_guess, 0)
    slopes(0)
    send_slab()
    load_source(0).wait()
    march(0, steps, (1,) if team > 2 else ())

    def from_end(x):
        @pl.when(first_block)
        def _():
            for f in range(fields):
                value = guess[0, f, x]
                state[0, x, f, body] = value
                relaxed[x, f] = value

        @pl.when(jnp.logical_not(first_block))
        def _():
            end_copy(0, x).wait_recv()
            for f in range(fields):
                value = end_in[0, x, f] + source[0, f, x]
                state[0, x, f, body] = value
                relaxed[x, f] = value

    begin(from_end)
    march(1, steps, range(2, team - 1))

    def last_slab():
        @pl.when(closes_team)
        def _():
            slab_copy(slabs_in.at[0], 0).wait_recv()

    def near(x):
        @pl.when(first_block)
        def _():
            for f in range(fields):
                value = source[0, f, x]
                residual_out[0, f, x] = value
                moved_in[x, f] = value

        @pl.when(jnp.logical_not(first_block))
        def _():
            end_copy(1, x).wait_recv()
            rest = []
            for f in range(fields):
                value = end_in[1, x, f] + source[0, f, x] - relaxed[x, f]
                residual_out[0, f, x] = value
                rest.append(value)

            @pl.when(member == 0)
            def _():
                for f in range(fields):
                    moved_in[x, f] = rest[f]

            @pl.when(member > 0)
            def _():
                err_copy(x).wait_recv()
                for f in range(fields):
                    moved_in[x, f] = moved_in[x, f] + rest[f]

        @pl.when(jnp.logical_not(closes_team))
        def _():
            error = coarse([scaled[0, f, x] for f in range(fields)],
                           [moved_in[x, f] for f in range(fields)])
            for f in range(fields):
                moved[x, f] = error[f]
            err_copy(x).start()

    def from_error(x):
        @pl.when(closes_team)
        def _():
            near(x)

        @pl.when(jnp.logical_not(first_team))
        def _():
            far_copy(x).wait_recv()

            def through(j, values):
                return tuple(coarse([slabs_in[j, f, x] for f in range(fields)], list(values)))

            values = lax.fori_loop(
                0, member, through, tuple(far_in[x, f] for f in range(fields)))
            for f in range(fields):
                moved_in[x, f] = moved_in[x, f] + values[f]

        error = [moved_in[x, f] for f in range(fields)]

        @pl.when(jnp.logical_and(closes_team, jnp.logical_not(last_team)))
        def _():
            going = coarse([scaled[0, f, x] for f in range(fields)], error)
            for f in range(fields):
                far_out[x, f] = going[f]
            far_copy(x).start()

        for b in reversed(range(depth)):
            @pl.when(jnp.logical_and(is_parent(b), jnp.logical_not(first_team)))
            def _():
                tree_copy(b, x).start()

        for f in range(fields):
            value = relaxed[x, f] + error[f]
            state[0, x, f, body] = value
            fine[0, f, x] = value

    last_slab()

    @pl.when(jnp.logical_not(closes_team))
    def _():
        near(0)
        near(last)

        def rest(x, carry):
            near(x)
            return carry

        lax.fori_loop(1, last, rest, 0)

    begin(from_error)
    store_fine(0).start()
    store_residual.start()
    march(2, steps - 1)

    for t in range(steps):
        store_fine(t).wait()
    store_residual.wait()

    def drain(x, carry):
        @pl.when(has_next)
        def _():
            end_copy(0, x).wait_send()
            end_copy(1, x).wait_send()

        @pl.when(jnp.logical_not(closes_team))
        def _():
            err_copy(x).wait_send()

        @pl.when(jnp.logical_and(closes_team, jnp.logical_not(last_team)))
        def _():
            far_copy(x).wait_send()

        for b in range(depth):
            @pl.when(jnp.logical_and(is_parent(b), jnp.logical_not(first_team)))
            def _():
                tree_copy(b, x).wait_send()
        return carry

    lax.fori_loop(0, nx, drain, 0)

    @pl.when(jnp.logical_not(closes_team))
    def _():
        def drain_slab(j, carry):
            slab_copy(slabs_in.at[j], j).wait_send()
            return carry

        lax.fori_loop(0, member, drain_slab, 0)
        slab_copy(scaled.at[0], member).wait_send()


def hand_out(fine, residual, fine_out, residual_out, fine_sem, residual_sem):
    copies = [pltpu.make_async_copy(fine.at[t], fine_out.at[t], fine_sem.at[t])
              for t in range(fine.shape[0])]
    copies.append(pltpu.make_async_copy(residual, residual_out, residual_sem))
    for copy in copies:
        copy.start()
    for copy in copies:
        copy.wait()


def per_device(blocks, slabs, primal, source, guess, mixing):
    steps, fields, nx, ny, nz = primal.shape
    groups = 2
    plane = (nx, fields, ny, nz)
    padded = (nx, fields, ny + 2 * PAD, nz)
    hbm = pl.BlockSpec(memory_space=pltpu.HBM)
    team = 2
    while (2 * team) ** 2 <= blocks and blocks % (2 * team) == 0:
        team *= 2
    dma = pltpu.SemaphoreType.DMA
    f32 = jnp.float32
    fine, residual = pl.pallas_call(
        functools.partial(kernel, blocks, slabs, team),
        out_shape=(jax.ShapeDtypeStruct(primal.shape, f32), jax.ShapeDtypeStruct(guess.shape, f32)),
        in_specs=[hbm] * 3 + [pl.BlockSpec(memory_space=pltpu.SMEM)],
        out_specs=(hbm, hbm),
        scratch_shapes=[
            pltpu.VMEM(primal.shape, f32),
            pltpu.VMEM(primal.shape, f32),
            pltpu.VMEM(guess.shape, f32),
            pltpu.VMEM(primal.shape, f32),
            pltpu.VMEM(guess.shape, f32),
            pltpu.VMEM(primal.shape, f32),
            pltpu.VMEM((2,) + padded, f32),
            pltpu.VMEM((2, 2, fields, ny, nz), f32),
            pltpu.VMEM((2,) + plane, f32),
            pltpu.VMEM((2,) + plane, f32),
            pltpu.VMEM(plane, f32),
            pltpu.VMEM(plane, f32),
            pltpu.VMEM(plane, f32),
            pltpu.VMEM((team - 1,) + primal.shape[1:], f32),
            pltpu.VMEM(plane, f32),
            pltpu.VMEM(plane, f32),
            dma((steps,)),
            dma((steps,)),
            dma,
            dma((steps,)),
            dma,
            dma((2, 2, groups)),
            dma((2, 2, groups)),
            dma((2, nx)),
            dma((2, nx)),
            dma((nx,)),
            dma((nx,)),
            dma((team,)),
            dma((team,)),
            dma((nx,)),
            dma((nx,)),
            dma((team.bit_length() - 1, nx)),
        ],
        compiler_params=pltpu.CompilerParams(
            collective_id=0, has_side_effects=True, vmem_limit_bytes=58 * 2**20),
    )(primal, source, guess, mixing)
    return pl.pallas_call(
        hand_out,
        out_shape=(jax.ShapeDtypeStruct(primal.shape, f32), jax.ShapeDtypeStruct(guess.shape, f32)),
        in_specs=[hbm] * 2,
        out_specs=(hbm, hbm),
        scratch_shapes=[dma((steps,)), dma],
        compiler_params=pltpu.CompilerParams(vmem_limit_bytes=58 * 2**20),
    )(fine, residual)


def solution(mesh):
    placed = P("tm", None, "space", None, None)
    return jax.shard_map(
        functools.partial(per_device, mesh.shape["tm"], mesh.shape["space"]),
        mesh=mesh,
        in_specs=(placed, placed, placed, P()),
        out_specs=(placed, placed),
        check_vma=False,
    )
```

```python
import functools

import jax
import jax.numpy as jnp
from jax import lax
from jax.experimental import pallas as pl
from jax.experimental.pallas import tpu as pltpu
from jax.sharding import PartitionSpec as P

DIFFUSION = 0.1
RATE = 0.25
COARSE_STEP = 0.75
KEEP = 1.0 - 6.0 * DIFFUSION - RATE
MESH = pl.DeviceIdType.MESH
LEFT, RIGHT = 0, 1
PAD = 8


def kernel(blocks, slabs, team, primal_hbm, source_hbm, guess_hbm, mixing, fine_hbm, residual_hbm,
           primal, source, guess, fine, residual_out, scaled, state, halo, ends, end_in, relaxed, moved, moved_in,
           slabs_in, far_in, far_out,
           load_p, load_s, load_g, store_f, store_r, halo_send, halo_recv, end_send, end_recv, err_send, err_recv,
           slab_send, slab_recv, far_send, far_recv, tree_send):
    steps, fields, nx, ny, nz = primal.shape
    last = nx - 1
    position = lax.axis_index("tm")
    slab = lax.axis_index("space")
    side = {LEFT: lax.rem(slab + slabs - 1, slabs), RIGHT: lax.rem(slab + 1, slabs)}
    edge = {LEFT: 0, RIGHT: last}
    first_block = position == 0
    has_next = position < blocks - 1
    member = lax.rem(position, team)
    closes_team = member == team - 1
    first_team = position < team
    last_team = position >= blocks - team
    depth = team.bit_length() - 1

    def is_parent(b):
        return lax.rem(position, 2 << b) == (2 << b) - 1

    def is_child(b):
        return lax.rem(position, 2 << b) == (1 << b) - 1
    groups = halo_send.shape[-1]
    cuts = [(g * fields) // groups for g in range(groups + 1)]

    def load_primal(t):
        return pltpu.make_async_copy(primal_hbm.at[t], primal.at[t], load_p.at[t])

    def load_source(t):
        return pltpu.make_async_copy(source_hbm.at[t], source.at[t], load_s.at[t])

    def store_fine(t):
        return pltpu.make_async_copy(fine.at[t], fine_hbm.at[t], store_f.at[t])

    store_residual = pltpu.make_async_copy(residual_out, residual_hbm, store_r)
    load_guess = pltpu.make_async_copy(guess_hbm, guess, load_g)
    load_guess.start()
    load_primal(0).start()
    load_source(0).start()
    for t in range(1, steps):
        load_source(t).start()
        load_primal(t).start()

    barrier = pltpu.get_barrier_semaphore()
    for way in (LEFT, RIGHT):
        pl.semaphore_signal(barrier, inc=1, device_id={"space": side[way]}, device_id_type=MESH)

    peers = [
        (jnp.logical_not(first_block), -1),
        (has_next, 1),
        (jnp.logical_and(closes_team, jnp.logical_not(first_team)), -team),
        (jnp.logical_and(closes_team, jnp.logical_not(last_team)), team),
    ]
    for b in range(depth):
        peers += [(is_parent(b), -(1 << b)), (is_child(b), 1 << b)]
    expected = 2
    for met, offset in peers:
        expected = expected + jnp.where(met, 1, 0)

        @pl.when(met)
        def _():
            pl.semaphore_signal(
                barrier, inc=1, device_id={"tm": position + offset}, device_id_type=MESH)

    pl.semaphore_wait(barrier, expected)

    weights = [[mixing[i, j] for j in range(fields)] for i in range(fields)]

    def mix(values, i):
        total = weights[i][0] * values[0]
        for j in range(1, fields):
            total = total + weights[i][j] * values[j]
        return total

    body = pl.ds(PAD, ny)
    blank = jnp.zeros((PAD, nz), jnp.float32)

    def clear(x, carry):
        for slot in range(2):
            for f in range(fields):
                state[slot, x, f, pl.ds(0, PAD)] = blank
                state[slot, x, f, pl.ds(PAD + ny, PAD)] = blank
        return carry

    lax.fori_loop(0, nx, clear, 0)

    def halo_copy(way, slot, g, given=False):
        part = pl.ds(cuts[g], cuts[g + 1] - cuts[g])
        return pltpu.make_async_remote_copy(
            src_ref=guess_hbm.at[0, part, edge[way]] if given
            else state.at[slot, edge[way], part, body],
            dst_ref=halo.at[way, slot, part],
            send_sem=halo_send.at[way, slot, g],
            recv_sem=halo_recv.at[way, slot, g],
            device_id={"space": side[way]},
            device_id_type=MESH,
        )

    def end_copy(m, x):
        return pltpu.make_async_remote_copy(
            src_ref=ends.at[m, x], dst_ref=end_in.at[m, x],
            send_sem=end_send.at[m, x], recv_sem=end_recv.at[m, x],
            device_id={"tm": position + 1}, device_id_type=MESH,
        )

    def pieces(x):
        cut = err_send.shape[-1] if isinstance(x, int) else 1
        return [(h, pl.ds(h * (ny // cut), ny // cut)) for h in range(cut)]

    def err_copy(x, h, part):
        return pltpu.make_async_remote_copy(
            src_ref=moved.at[x, :, part], dst_ref=moved_in.at[x, :, part],
            send_sem=err_send.at[x, h], recv_sem=err_recv.at[x, h],
            device_id={"tm": position + 1}, device_id_type=MESH,
        )

    def slab_copy(src, j):
        return pltpu.make_async_remote_copy(
            src_ref=src, dst_ref=slabs_in.at[j],
            send_sem=slab_send.at[j], recv_sem=slab_recv.at[j],
            device_id={"tm": position + 1}, device_id_type=MESH,
        )

    def far_copy(x, h, part):
        return pltpu.make_async_remote_copy(
            src_ref=far_out.at[x, :, part], dst_ref=far_in.at[x, :, part],
            send_sem=far_send.at[x, h], recv_sem=far_recv.at[x, h],
            device_id={"tm": position + team}, device_id_type=MESH,
        )

    def tree_copy(b, x, h, part):
        return pltpu.make_async_remote_copy(
            src_ref=far_in.at[x, :, part], dst_ref=far_in.at[x, :, part],
            send_sem=tree_send.at[b, x, h], recv_sem=far_recv.at[x, h],
            device_id={"tm": position - (1 << b)}, device_id_type=MESH,
        )

    def send_slab():
        @pl.when(jnp.logical_not(closes_team))
        def _():
            slab_copy(scaled.at[0], member).start()

    def pass_slab(hop):
        @pl.when(member >= hop)
        def _():
            j = member - hop
            slab_copy(slabs_in.at[j], j).wait_recv()

            @pl.when(jnp.logical_not(closes_team))
            def _():
                slab_copy(slabs_in.at[j], j).start()

    def slopes(t):
        load_primal(t).wait()

        def slope(x, carry):
            values = [primal[t, f, x] for f in range(fields)]
            for f in range(fields):
                bent = jnp.tanh(mix(values, f))
                scaled[t, f, x] = RATE - RATE * (bent * bent)
            return carry

        lax.fori_loop(0, nx, slope, 0, unroll=2)

    def coarse(slope, values):
        return [(1.0 - COARSE_STEP) * values[f]
                + (COARSE_STEP / RATE) * (slope[f] * mix(values, f)) for f in range(fields)]

    def stepped(slot, t, x, near):
        values = [state[slot, x, f, body] for f in range(fields)]
        results = []
        for f in range(fields):
            v = values[f]
            around = pltpu.roll(v, 1, 1) + pltpu.roll(v, nz - 1, 1)
            around = around + state[slot, x, f, pl.ds(PAD - 1, ny)]
            around = around + state[slot, x, f, pl.ds(PAD + 1, ny)]
            for other in near:
                around = around + state[slot, other, f, body]
            results.append(KEEP * v + DIFFUSION * around + scaled[t, f, x] * mix(values, f))
        return results

    early = (1, last - 1)

    def step(m, slot, t, ways, closing):
        final = m == 2

        def given(x, f, value):
            return value if closing and not final else value + source[t + 1, f, x]

        def put(x, f, value):
            if closing and not final:
                ends[m, x, f] = value
                return
            if final:
                fine[t + 1, f, x] = value
            if not closing:
                state[1 - slot, x, f, body] = value

        if m == 0 and not closing:
            load_source(t + 1).wait()
            slopes(t + 1)

        def inner(x):
            results = stepped(slot, t, x, (x - 1, x + 1))
            for f in range(fields):
                put(x, f, given(x, f, results[f]))

        for x in range(1, last):
            inner(x)
            if closing and not final and x in early:
                @pl.when(has_next)
                def _():
                    end_copy(m, x).start()
        waiting = []
        for way in ways:
            target = RIGHT if way == LEFT else LEFT
            x = edge[target]
            results = stepped(slot, t, x, (x + 1 if target == LEFT else x - 1,))
            waiting.append((way, target, x, [given(x, f, results[f]) for f in range(fields)]))
        for way, target, x, results in waiting:
            for g in range(groups):
                halo_copy(way, slot, g).wait_recv()
                for f in range(cuts[g], cuts[g + 1]):
                    put(x, f, results[f] + DIFFUSION * halo[way, slot, f])
                if not closing:
                    halo_copy(target, 1 - slot, g).start()
            if closing and not final:
                @pl.when(has_next)
                def _():
                    end_copy(m, x).start()
        if closing and not final:
            @pl.when(has_next)
            def _():
                for x in range(1, last):
                    if x not in early:
                        end_copy(m, x).start()
        for way in ways:
            for g in range(groups):
                halo_copy(way, slot, g).wait_send()
        if final:
            store_fine(t + 1).start()

    forward, backward = (LEFT, RIGHT), (RIGHT, LEFT)

    def march(m, count, between=()):
        pairs = (count - 1) // 2

        def pair(i, carry):
            step(m, 0, 2 * i, forward, False)
            step(m, 1, 2 * i + 1, backward, False)
            return carry

        lax.fori_loop(0, pairs, pair, 0)
        for hop in between:
            pass_slab(hop)
        for t in range(2 * pairs, count):
            step(m, t % 2, t, (forward, backward)[t % 2], t == count - 1)

    def send_edge(way):
        for g in range(groups):
            halo_copy(way, 0, g).start()

    def begin(place):
        place(edge[LEFT])
        send_edge(LEFT)
        place(edge[RIGHT])
        send_edge(RIGHT)

        def rest(x, carry):
            place(x)
            return carry

        lax.fori_loop(1, last, rest, 0)

    def from_guess(x):
        for f in range(fields):
            state[0, x, f, body] = guess[0, f, x]

    for way in (LEFT, RIGHT):
        for g in range(groups):
            halo_copy(way, 0, g, True).start()
    load_guess.wait()

    def copy_guess(x, carry):
        from_guess(x)
        return carry

    lax.fori_loop(0, nx, copy_guess, 0)
    slopes(0)
    send_slab()
    load_source(0).wait()
    march(0, steps, (1,) if team > 2 else ())

    def from_end(x):
        @pl.when(first_block)
        def _():
            for f in range(fields):
                value = guess[0, f, x]
                state[0, x, f, body] = value
                relaxed[x, f] = value

        @pl.when(jnp.logical_not(first_block))
        def _():
            end_copy(0, x).wait_recv()
            for f in range(fields):
                value = end_in[0, x, f] + source[0, f, x]
                state[0, x, f, body] = value
                relaxed[x, f] = value

    begin(from_end)
    march(1, steps, range(2, team - 1))

    def last_slab():
        @pl.when(closes_team)
        def _():
            slab_copy(slabs_in.at[0], 0).wait_recv()

    def arrived(x):
        @pl.when(jnp.logical_not(first_block))
        def _():
            end_copy(1, x).wait_recv()

    def near(x, h, part):
        @pl.when(first_block)
        def _():
            for f in range(fields):
                value = source[0, f, x, part]
                residual_out[0, f, x, part] = value
                moved_in[x, f, part] = value

        @pl.when(jnp.logical_not(first_block))
        def _():
            rest = []
            for f in range(fields):
                value = end_in[1, x, f, part] + source[0, f, x, part] - relaxed[x, f, part]
                residual_out[0, f, x, part] = value
                rest.append(value)

            @pl.when(member == 0)
            def _():
                for f in range(fields):
                    moved_in[x, f, part] = rest[f]

            @pl.when(member > 0)
            def _():
                err_copy(x, h, part).wait_recv()
                for f in range(fields):
                    moved_in[x, f, part] = moved_in[x, f, part] + rest[f]

        @pl.when(jnp.logical_not(closes_team))
        def _():
            error = coarse([scaled[0, f, x, part] for f in range(fields)],
                           [moved_in[x, f, part] for f in range(fields)])
            for f in range(fields):
                moved[x, f, part] = error[f]
            err_copy(x, h, part).start()

    def near_plane(x):
        arrived(x)
        for h, part in pieces(x):
            near(x, h, part)

    def from_error(x):
        @pl.when(closes_team)
        def _():
            arrived(x)

        for h, part in pieces(x):
            corrected(x, h, part)

    def corrected(x, h, part):
        @pl.when(closes_team)
        def _():
            near(x, h, part)

        @pl.when(jnp.logical_not(first_team))
        def _():
            far_copy(x, h, part).wait_recv()

            def through(j, values):
                return tuple(
                    coarse([slabs_in[j, f, x, part] for f in range(fields)], list(values)))

            values = lax.fori_loop(
                0, member, through, tuple(far_in[x, f, part] for f in range(fields)))
            for f in range(fields):
                moved_in[x, f, part] = moved_in[x, f, part] + values[f]

        error = [moved_in[x, f, part] for f in range(fields)]

        @pl.when(jnp.logical_and(closes_team, jnp.logical_not(last_team)))
        def _():
            going = coarse([scaled[0, f, x, part] for f in range(fields)], error)
            for f in range(fields):
                far_out[x, f, part] = going[f]
            far_copy(x, h, part).start()

        for b in reversed(range(depth)):
            @pl.when(jnp.logical_and(is_parent(b), jnp.logical_not(first_team)))
            def _():
                tree_copy(b, x, h, part).start()

        for f in range(fields):
            value = relaxed[x, f, part] + error[f]
            state[0, x, f, pl.ds(PAD + part.start, part.size)] = value
            fine[0, f, x, part] = value

    last_slab()

    @pl.when(jnp.logical_not(closes_team))
    def _():
        near_plane(0)
        near_plane(last)

        def rest(x, carry):
            near_plane(x)
            return carry

        lax.fori_loop(1, last, rest, 0)

    begin(from_error)
    store_fine(0).start()
    store_residual.start()
    march(2, steps - 1)

    for t in range(steps):
        store_fine(t).wait()
    store_residual.wait()

    def drain(x, carry):
        @pl.when(has_next)
        def _():
            end_copy(0, x).wait_send()
            end_copy(1, x).wait_send()

        for h, part in pieces(x):
            @pl.when(jnp.logical_not(closes_team))
            def _():
                err_copy(x, h, part).wait_send()

            @pl.when(jnp.logical_and(closes_team, jnp.logical_not(last_team)))
            def _():
                far_copy(x, h, part).wait_send()

            for b in range(depth):
                @pl.when(jnp.logical_and(is_parent(b), jnp.logical_not(first_team)))
                def _():
                    tree_copy(b, x, h, part).wait_send()
        return carry

    drain(0, 0)
    drain(last, 0)
    lax.fori_loop(1, last, drain, 0)

    @pl.when(jnp.logical_not(closes_team))
    def _():
        def drain_slab(j, carry):
            slab_copy(slabs_in.at[j], j).wait_send()
            return carry

        lax.fori_loop(0, member, drain_slab, 0)
        slab_copy(scaled.at[0], member).wait_send()


def hand_out(fine, residual, fine_out, residual_out, fine_held, residual_held,
             fine_in, fine_sem, residual_in, residual_sem):
    pieces = [(fine.at[t], fine_held.at[t], fine_out.at[t], fine_in.at[t], fine_sem.at[t])
              for t in range(fine.shape[0])]
    pieces.append((residual, residual_held, residual_out, residual_in, residual_sem))
    loads = [pltpu.make_async_copy(src, held, sem) for src, held, _, sem, _ in pieces]
    stores = [pltpu.make_async_copy(held, dst, sem) for _, held, dst, _, sem in pieces]
    for load in loads:
        load.start()
    for load, store in zip(loads, stores):
        load.wait()
        store.start()
    for store in stores:
        store.wait()


def per_device(blocks, slabs, primal, source, guess, mixing):
    steps, fields, nx, ny, nz = primal.shape
    groups = 2
    halves = 2 if ny % 16 == 0 else 1
    plane = (nx, fields, ny, nz)
    padded = (nx, fields, ny + 2 * PAD, nz)
    hbm = pl.BlockSpec(memory_space=pltpu.HBM)
    team = 2
    while (2 * team) ** 2 <= blocks and blocks % (2 * team) == 0:
        team *= 2
    dma = pltpu.SemaphoreType.DMA
    f32 = jnp.float32
    fine, residual = pl.pallas_call(
        functools.partial(kernel, blocks, slabs, team),
        out_shape=(jax.ShapeDtypeStruct(primal.shape, f32), jax.ShapeDtypeStruct(guess.shape, f32)),
        in_specs=[hbm] * 3 + [pl.BlockSpec(memory_space=pltpu.SMEM)],
        out_specs=(hbm, hbm),
        scratch_shapes=[
            pltpu.VMEM(primal.shape, f32),
            pltpu.VMEM(primal.shape, f32),
            pltpu.VMEM(guess.shape, f32),
            pltpu.VMEM(primal.shape, f32),
            pltpu.VMEM(guess.shape, f32),
            pltpu.VMEM(primal.shape, f32),
            pltpu.VMEM((2,) + padded, f32),
            pltpu.VMEM((2, 2, fields, ny, nz), f32),
            pltpu.VMEM((2,) + plane, f32),
            pltpu.VMEM((2,) + plane, f32),
            pltpu.VMEM(plane, f32),
            pltpu.VMEM(plane, f32),
            pltpu.VMEM(plane, f32),
            pltpu.VMEM((team - 1,) + primal.shape[1:], f32),
            pltpu.VMEM(plane, f32),
            pltpu.VMEM(plane, f32),
            dma((steps,)),
            dma((steps,)),
            dma,
            dma((steps,)),
            dma,
            dma((2, 2, groups)),
            dma((2, 2, groups)),
            dma((2, nx)),
            dma((2, nx)),
            dma((nx, halves)),
            dma((nx, halves)),
            dma((team,)),
            dma((team,)),
            dma((nx, halves)),
            dma((nx, halves)),
            dma((team.bit_length() - 1, nx, halves)),
        ],
        compiler_params=pltpu.CompilerParams(
            collective_id=0, has_side_effects=True, vmem_limit_bytes=58 * 2**20),
    )(primal, source, guess, mixing)
    return pl.pallas_call(
        hand_out,
        out_shape=(jax.ShapeDtypeStruct(primal.shape, f32), jax.ShapeDtypeStruct(guess.shape, f32)),
        in_specs=[hbm] * 2,
        out_specs=(hbm, hbm),
        scratch_shapes=[
            pltpu.VMEM(primal.shape, f32),
            pltpu.VMEM(guess.shape, f32),
            dma((steps,)),
            dma((steps,)),
            dma,
            dma,
        ],
        compiler_params=pltpu.CompilerParams(vmem_limit_bytes=58 * 2**20),
    )(fine, residual)


def solution(mesh):
    placed = P("tm", None, "space", None, None)
    return jax.shard_map(
        functools.partial(per_device, mesh.shape["tm"], mesh.shape["space"]),
        mesh=mesh,
        in_specs=(placed, placed, placed, P()),
        out_specs=(placed, placed),
        check_vma=False,
    )
```

```python
import functools

import jax
import jax.numpy as jnp
from jax import lax
from jax.experimental import pallas as pl
from jax.experimental.pallas import tpu as pltpu
from jax.sharding import PartitionSpec as P

DIFFUSION = 0.1
RATE = 0.25
COARSE_STEP = 0.75
KEEP = 1.0 - 6.0 * DIFFUSION - RATE
MESH = pl.DeviceIdType.MESH
LEFT, RIGHT = 0, 1
PAD = 8


def kernel(blocks, slabs, team, primal_hbm, source_hbm, guess_hbm, mixing, fine_hbm, residual_hbm,
           primal, source, guess, fine, residual_out, scaled, state, halo, ends, end_in, relaxed, moved, moved_in,
           slabs_in, far_in, far_out,
           load_p, load_s, load_g, store_f, store_r, halo_send, halo_recv, end_send, end_recv, err_send, err_recv,
           slab_send, slab_recv, far_send, far_recv, tree_send):
    steps, fields, nx, ny, nz = primal.shape
    last = nx - 1
    position = lax.axis_index("tm")
    slab = lax.axis_index("space")
    side = {LEFT: lax.rem(slab + slabs - 1, slabs), RIGHT: lax.rem(slab + 1, slabs)}
    edge = {LEFT: 0, RIGHT: last}
    first_block = position == 0
    has_next = position < blocks - 1
    member = lax.rem(position, team)
    closes_team = member == team - 1
    first_team = position < team
    last_team = position >= blocks - team
    depth = team.bit_length() - 1

    def is_parent(b):
        return lax.rem(position, 2 << b) == (2 << b) - 1

    def is_child(b):
        return lax.rem(position, 2 << b) == (1 << b) - 1
    groups = halo_send.shape[-1]
    cuts = [(g * fields) // groups for g in range(groups + 1)]

    def load_primal(t):
        return pltpu.make_async_copy(primal_hbm.at[t], primal.at[t], load_p.at[t])

    def load_source(t):
        return pltpu.make_async_copy(source_hbm.at[t], source.at[t], load_s.at[t])

    def store_fine(t):
        return pltpu.make_async_copy(fine.at[t], fine_hbm.at[t], store_f.at[t])

    store_residual = pltpu.make_async_copy(residual_out, residual_hbm, store_r)
    load_guess = pltpu.make_async_copy(guess_hbm, guess, load_g)
    load_guess.start()
    load_primal(0).start()
    load_source(0).start()
    for t in range(1, steps):
        load_source(t).start()
        load_primal(t).start()

    barrier = pltpu.get_barrier_semaphore()
    for way in (LEFT, RIGHT):
        pl.semaphore_signal(barrier, inc=1, device_id={"space": side[way]}, device_id_type=MESH)

    peers = [
        (jnp.logical_not(first_block), -1),
        (has_next, 1),
        (jnp.logical_and(closes_team, jnp.logical_not(first_team)), -team),
        (jnp.logical_and(closes_team, jnp.logical_not(last_team)), team),
    ]
    for b in range(depth):
        peers += [(is_parent(b), -(1 << b)), (is_child(b), 1 << b)]
    expected = 2
    for met, offset in peers:
        expected = expected + jnp.where(met, 1, 0)

        @pl.when(met)
        def _():
            pl.semaphore_signal(
                barrier, inc=1, device_id={"tm": position + offset}, device_id_type=MESH)

    pl.semaphore_wait(barrier, expected)

    weights = [[mixing[i, j] for j in range(fields)] for i in range(fields)]

    def mix(values, i):
        total = weights[i][0] * values[0]
        for j in range(1, fields):
            total = total + weights[i][j] * values[j]
        return total

    body = pl.ds(PAD, ny)
    blank = jnp.zeros((PAD, nz), jnp.float32)

    def clear(x, carry):
        for slot in range(2):
            for f in range(fields):
                state[slot, x, f, pl.ds(0, PAD)] = blank
                state[slot, x, f, pl.ds(PAD + ny, PAD)] = blank
        return carry

    lax.fori_loop(0, nx, clear, 0)

    def halo_copy(way, slot, g, given=False):
        part = pl.ds(cuts[g], cuts[g + 1] - cuts[g])
        return pltpu.make_async_remote_copy(
            src_ref=guess_hbm.at[0, part, edge[way]] if given
            else state.at[slot, edge[way], part, body],
            dst_ref=halo.at[way, slot, part],
            send_sem=halo_send.at[way, slot, g],
            recv_sem=halo_recv.at[way, slot, g],
            device_id={"space": side[way]},
            device_id_type=MESH,
        )

    def end_copy(m, x):
        return pltpu.make_async_remote_copy(
            src_ref=ends.at[m, x], dst_ref=end_in.at[m, x],
            send_sem=end_send.at[m, x], recv_sem=end_recv.at[m, x],
            device_id={"tm": position + 1}, device_id_type=MESH,
        )

    def pieces(x):
        cut = err_send.shape[-1] if isinstance(x, int) else 1
        return [(h, pl.ds(h * (ny // cut), ny // cut)) for h in range(cut)]

    def err_copy(x, h, part):
        return pltpu.make_async_remote_copy(
            src_ref=moved.at[x, :, part], dst_ref=moved_in.at[x, :, part],
            send_sem=err_send.at[x, h], recv_sem=err_recv.at[x, h],
            device_id={"tm": position + 1}, device_id_type=MESH,
        )

    def slab_copy(src, j):
        return pltpu.make_async_remote_copy(
            src_ref=src, dst_ref=slabs_in.at[j],
            send_sem=slab_send.at[j], recv_sem=slab_recv.at[j],
            device_id={"tm": position + 1}, device_id_type=MESH,
        )

    def far_copy(x, h, part):
        return pltpu.make_async_remote_copy(
            src_ref=far_out.at[x, :, part], dst_ref=far_in.at[x, :, part],
            send_sem=far_send.at[x, h], recv_sem=far_recv.at[x, h],
            device_id={"tm": position + team}, device_id_type=MESH,
        )

    def tree_copy(b, x, h, part):
        return pltpu.make_async_remote_copy(
            src_ref=far_in.at[x, :, part], dst_ref=far_in.at[x, :, part],
            send_sem=tree_send.at[b, x, h], recv_sem=far_recv.at[x, h],
            device_id={"tm": position - (1 << b)}, device_id_type=MESH,
        )

    def send_slab():
        @pl.when(jnp.logical_not(closes_team))
        def _():
            slab_copy(scaled.at[0], member).start()

    def pass_slab(hop):
        @pl.when(member >= hop)
        def _():
            j = member - hop
            slab_copy(slabs_in.at[j], j).wait_recv()

            @pl.when(jnp.logical_not(closes_team))
            def _():
                slab_copy(slabs_in.at[j], j).start()

    def slopes(t):
        load_primal(t).wait()

        def slope(x, carry):
            values = [primal[t, f, x] for f in range(fields)]
            for f in range(fields):
                bent = jnp.tanh(mix(values, f))
                scaled[t, f, x] = RATE - RATE * (bent * bent)
            return carry

        lax.fori_loop(0, nx, slope, 0, unroll=2)

    def coarse(slope, values):
        return [(1.0 - COARSE_STEP) * values[f]
                + (COARSE_STEP / RATE) * (slope[f] * mix(values, f)) for f in range(fields)]

    def stepped(slot, t, x, near):
        values = [state[slot, x, f, body] for f in range(fields)]
        results = []
        for f in range(fields):
            v = values[f]
            around = pltpu.roll(v, 1, 1) + pltpu.roll(v, nz - 1, 1)
            around = around + state[slot, x, f, pl.ds(PAD - 1, ny)]
            around = around + state[slot, x, f, pl.ds(PAD + 1, ny)]
            for other in near:
                around = around + state[slot, other, f, body]
            results.append(KEEP * v + DIFFUSION * around + scaled[t, f, x] * mix(values, f))
        return results

    early = (1, last - 1)

    def step(m, slot, t, ways, closing):
        final = m == 2

        def given(x, f, value):
            return value if closing and not final else value + source[t + 1, f, x]

        def put(x, f, value):
            if closing and not final:
                ends[m, x, f] = value
                return
            if final:
                fine[t + 1, f, x] = value
            if not closing:
                state[1 - slot, x, f, body] = value

        if m == 0 and not closing:
            load_source(t + 1).wait()
            slopes(t + 1)

        def inner(x):
            results = stepped(slot, t, x, (x - 1, x + 1))
            for f in range(fields):
                put(x, f, given(x, f, results[f]))

        for x in range(1, last):
            inner(x)
            if closing and not final and x in early:
                @pl.when(has_next)
                def _():
                    end_copy(m, x).start()
        waiting = []
        for way in ways:
            target = RIGHT if way == LEFT else LEFT
            x = edge[target]
            results = stepped(slot, t, x, (x + 1 if target == LEFT else x - 1,))
            waiting.append((way, target, x, [given(x, f, results[f]) for f in range(fields)]))
        for way, target, x, results in waiting:
            for g in range(groups):
                halo_copy(way, slot, g).wait_recv()
                for f in range(cuts[g], cuts[g + 1]):
                    put(x, f, results[f] + DIFFUSION * halo[way, slot, f])
                if not closing:
                    halo_copy(target, 1 - slot, g).start()
            if closing and not final:
                @pl.when(has_next)
                def _():
                    end_copy(m, x).start()
        if closing and not final:
            @pl.when(has_next)
            def _():
                for x in range(1, last):
                    if x not in early:
                        end_copy(m, x).start()
        for way in ways:
            for g in range(groups):
                halo_copy(way, slot, g).wait_send()
        if final:
            store_fine(t + 1).start()

    forward, backward = (LEFT, RIGHT), (RIGHT, LEFT)

    def march(m, count, between=()):
        pairs = (count - 1) // 2

        def pair(i, carry):
            step(m, 0, 2 * i, forward, False)
            step(m, 1, 2 * i + 1, backward, False)
            return carry

        lax.fori_loop(0, pairs, pair, 0)
        for hop in between:
            pass_slab(hop)
        for t in range(2 * pairs, count):
            step(m, t % 2, t, (forward, backward)[t % 2], t == count - 1)

    def send_edge(way):
        for g in range(groups):
            halo_copy(way, 0, g).start()

    def begin(place):
        place(edge[LEFT])
        send_edge(LEFT)
        place(edge[RIGHT])
        send_edge(RIGHT)

        def rest(x, carry):
            place(x)
            return carry

        lax.fori_loop(1, last, rest, 0)

    def from_guess(x):
        for f in range(fields):
            state[0, x, f, body] = guess[0, f, x]

    for way in (LEFT, RIGHT):
        for g in range(groups):
            halo_copy(way, 0, g, True).start()
    load_guess.wait()

    def copy_guess(x, carry):
        from_guess(x)
        return carry

    lax.fori_loop(0, nx, copy_guess, 0)
    slopes(0)
    send_slab()
    load_source(0).wait()
    march(0, steps, (1,) if team > 2 else ())

    def from_end(x):
        @pl.when(first_block)
        def _():
            for f in range(fields):
                value = guess[0, f, x]
                state[0, x, f, body] = value
                relaxed[x, f] = value

        @pl.when(jnp.logical_not(first_block))
        def _():
            end_copy(0, x).wait_recv()
            for f in range(fields):
                value = end_in[0, x, f] + source[0, f, x]
                state[0, x, f, body] = value
                relaxed[x, f] = value

    begin(from_end)
    march(1, steps, range(2, team - 1))

    def last_slab():
        @pl.when(closes_team)
        def _():
            slab_copy(slabs_in.at[0], 0).wait_recv()

    def arrived(x):
        @pl.when(jnp.logical_not(first_block))
        def _():
            end_copy(1, x).wait_recv()

    def near(x, h, part):
        @pl.when(first_block)
        def _():
            for f in range(fields):
                value = source[0, f, x, part]
                residual_out[0, f, x, part] = value
                moved_in[x, f, part] = value

        @pl.when(jnp.logical_not(first_block))
        def _():
            rest = []
            for f in range(fields):
                value = end_in[1, x, f, part] + source[0, f, x, part] - relaxed[x, f, part]
                residual_out[0, f, x, part] = value
                rest.append(value)

            @pl.when(member == 0)
            def _():
                for f in range(fields):
                    moved_in[x, f, part] = rest[f]

            @pl.when(member > 0)
            def _():
                err_copy(x, h, part).wait_recv()
                for f in range(fields):
                    moved_in[x, f, part] = moved_in[x, f, part] + rest[f]

        @pl.when(jnp.logical_not(closes_team))
        def _():
            error = coarse([scaled[0, f, x, part] for f in range(fields)],
                           [moved_in[x, f, part] for f in range(fields)])
            for f in range(fields):
                moved[x, f, part] = error[f]
            err_copy(x, h, part).start()

    def near_plane(x):
        arrived(x)
        for h, part in pieces(x):
            near(x, h, part)

    def from_error(x):
        @pl.when(closes_team)
        def _():
            arrived(x)

        for h, part in pieces(x):
            corrected(x, h, part)

    def corrected(x, h, part):
        @pl.when(closes_team)
        def _():
            near(x, h, part)

        @pl.when(jnp.logical_not(first_team))
        def _():
            far_copy(x, h, part).wait_recv()

            def through(j, values):
                return tuple(
                    coarse([slabs_in[j, f, x, part] for f in range(fields)], list(values)))

            values = lax.fori_loop(
                0, member, through, tuple(far_in[x, f, part] for f in range(fields)))
            for f in range(fields):
                moved_in[x, f, part] = moved_in[x, f, part] + values[f]

        error = [moved_in[x, f, part] for f in range(fields)]

        @pl.when(jnp.logical_and(closes_team, jnp.logical_not(last_team)))
        def _():
            going = coarse([scaled[0, f, x, part] for f in range(fields)], error)
            for f in range(fields):
                far_out[x, f, part] = going[f]
            far_copy(x, h, part).start()

        for b in reversed(range(depth)):
            @pl.when(jnp.logical_and(is_parent(b), jnp.logical_not(first_team)))
            def _():
                tree_copy(b, x, h, part).start()

        for f in range(fields):
            value = relaxed[x, f, part] + error[f]
            state[0, x, f, pl.ds(PAD + part.start, part.size)] = value
            fine[0, f, x, part] = value

    last_slab()

    @pl.when(jnp.logical_not(closes_team))
    def _():
        near_plane(0)
        near_plane(last)

        def rest(x, carry):
            near_plane(x)
            return carry

        lax.fori_loop(1, last, rest, 0)

    begin(from_error)
    store_fine(0).start()
    store_residual.start()
    march(2, steps - 1)

    for t in range(steps):
        store_fine(t).wait()
    store_residual.wait()

    def drain(x, carry):
        @pl.when(has_next)
        def _():
            end_copy(0, x).wait_send()
            end_copy(1, x).wait_send()

        for h, part in pieces(x):
            @pl.when(jnp.logical_not(closes_team))
            def _():
                err_copy(x, h, part).wait_send()

            @pl.when(jnp.logical_and(closes_team, jnp.logical_not(last_team)))
            def _():
                far_copy(x, h, part).wait_send()

            for b in range(depth):
                @pl.when(jnp.logical_and(is_parent(b), jnp.logical_not(first_team)))
                def _():
                    tree_copy(b, x, h, part).wait_send()
        return carry

    drain(0, 0)
    drain(last, 0)
    lax.fori_loop(1, last, drain, 0)

    @pl.when(jnp.logical_not(closes_team))
    def _():
        def drain_slab(j, carry):
            slab_copy(slabs_in.at[j], j).wait_send()
            return carry

        lax.fori_loop(0, member, drain_slab, 0)
        slab_copy(scaled.at[0], member).wait_send()


def hand_out(fine, residual, fine_out, residual_out, fine_held, residual_held,
             fine_in, fine_sem, residual_in, residual_sem):
    pieces = [(fine.at[t], fine_held.at[t], fine_out.at[t], fine_in.at[t], fine_sem.at[t])
              for t in range(fine.shape[0])]
    pieces.append((residual, residual_held, residual_out, residual_in, residual_sem))
    loads = [pltpu.make_async_copy(src, held, sem) for src, held, _, sem, _ in pieces]
    stores = [pltpu.make_async_copy(held, dst, sem) for _, held, dst, _, sem in pieces]
    for load in loads:
        load.start()
    for load, store in zip(loads, stores):
        load.wait()
        store.start()
    for store in stores:
        store.wait()


def per_device(blocks, slabs, primal, source, guess, mixing):
    steps, fields, nx, ny, nz = primal.shape
    groups = fields
    halves = 1
    plane = (nx, fields, ny, nz)
    padded = (nx, fields, ny + 2 * PAD, nz)
    hbm = pl.BlockSpec(memory_space=pltpu.HBM)
    team = 2
    while (2 * team) ** 2 <= blocks and blocks % (2 * team) == 0:
        team *= 2
    dma = pltpu.SemaphoreType.DMA
    f32 = jnp.float32
    fine, residual = pl.pallas_call(
        functools.partial(kernel, blocks, slabs, team),
        out_shape=(jax.ShapeDtypeStruct(primal.shape, f32), jax.ShapeDtypeStruct(guess.shape, f32)),
        in_specs=[hbm] * 3 + [pl.BlockSpec(memory_space=pltpu.SMEM)],
        out_specs=(hbm, hbm),
        scratch_shapes=[
            pltpu.VMEM(primal.shape, f32),
            pltpu.VMEM(primal.shape, f32),
            pltpu.VMEM(guess.shape, f32),
            pltpu.VMEM(primal.shape, f32),
            pltpu.VMEM(guess.shape, f32),
            pltpu.VMEM(primal.shape, f32),
            pltpu.VMEM((2,) + padded, f32),
            pltpu.VMEM((2, 2, fields, ny, nz), f32),
            pltpu.VMEM((2,) + plane, f32),
            pltpu.VMEM((2,) + plane, f32),
            pltpu.VMEM(plane, f32),
            pltpu.VMEM(plane, f32),
            pltpu.VMEM(plane, f32),
            pltpu.VMEM((team - 1,) + primal.shape[1:], f32),
            pltpu.VMEM(plane, f32),
            pltpu.VMEM(plane, f32),
            dma((steps,)),
            dma((steps,)),
            dma,
            dma((steps,)),
            dma,
            dma((2, 2, groups)),
            dma((2, 2, groups)),
            dma((2, nx)),
            dma((2, nx)),
            dma((nx, halves)),
            dma((nx, halves)),
            dma((team,)),
            dma((team,)),
            dma((nx, halves)),
            dma((nx, halves)),
            dma((team.bit_length() - 1, nx, halves)),
        ],
        compiler_params=pltpu.CompilerParams(
            collective_id=0, has_side_effects=True, vmem_limit_bytes=58 * 2**20),
    )(primal, source, guess, mixing)
    return pl.pallas_call(
        hand_out,
        out_shape=(jax.ShapeDtypeStruct(primal.shape, f32), jax.ShapeDtypeStruct(guess.shape, f32)),
        in_specs=[hbm] * 2,
        out_specs=(hbm, hbm),
        scratch_shapes=[
            pltpu.VMEM(primal.shape, f32),
            pltpu.VMEM(guess.shape, f32),
            dma((steps,)),
            dma((steps,)),
            dma,
            dma,
        ],
        compiler_params=pltpu.CompilerParams(vmem_limit_bytes=58 * 2**20),
    )(fine, residual)


def solution(mesh):
    placed = P("tm", None, "space", None, None)
    return jax.shard_map(
        functools.partial(per_device, mesh.shape["tm"], mesh.shape["space"]),
        mesh=mesh,
        in_specs=(placed, placed, placed, P()),
        out_specs=(placed, placed),
        check_vma=False,
    )
```
